512 devices in a mesh: dp: 32 (over y, x), shard: 16 (over z, core).
Axes of the slice: x: 4, y: 8, z: 8, core: 2. Of those that a mesh axis runs over, the one named last changes fastest.
Arguments:
- partials: bfloat16 [32, 128, 256, 256], P('dp', 'shard'), may hold values from -6 to 6
- params: float32 [128, 256, 256], P('shard', 'dp'), may hold values from -0.75 to 0.75
- left_basis: float32 [32, 16, 1, 256, 256], P('dp', 'shard'), may hold values from -0.375 to 0.375
- right_basis: float32 [32, 16, 1, 256, 256], P('dp', 'shard'), may hold values from -0.375 to 0.375
- first_moment: float32 [32, 16, 1, 256, 256], P('dp', 'shard'), may hold values from -4 to 4
- second_moment: float32 [32, 16, 1, 256, 256], P('dp', 'shard'), may hold values from 0.1 to 10
- owner_list: int32 [128], replicated, may hold values from 0 to 511, as said below
Outputs:
- updated: float32 [128, 256, 256], P('shard')
- first_out: float32 [32, 16, 1, 256, 256], P('dp', 'shard')
- second_out: float32 [32, 16, 1, 256, 256], P('dp', 'shard')
The draws below stay inside these ranges and needn't reach their ends.
Inputs may be any that keep to these rules, and one draw needn't show every extreme that they name: `owner_list`: each owner device is named by at most 1 block, and some device by exactly 1.
All inputs are finite; a program needn't handle non-finite values.
Results may differ from the reference program's by a relative error of at most 0.0003.
Values sent between devices are 32-bit elements; how exact they have to be, the bound alone decides.
A program may use at most 64 MiB of HBM per device.

```python
import math
import jax
import jax.numpy as jnp
from jax import lax

BLK = 256
CAP = 1
BLOCKS = 128
N_DP = 32
N_SHARD = 16


def draw_owner_list(key, part):
    order_key = jax.random.fold_in(key, 202)
    device_total = N_DP * N_SHARD
    return jax.random.permutation(order_key, device_total).astype(jnp.int32)[:BLOCKS]


def raised(values, stream_key, source, target, blocks, factor):
    def block_of(position):
        return (jnp.arange(values.shape[position]) // (values.shape[position] // blocks)).reshape((-1,) + (1,) * (values.ndim - 1 - position))

    first = jax.random.permutation(stream_key, blocks)[block_of(target)]
    far = (block_of(target) + blocks // 2) % blocks
    return jnp.where((block_of(source) == first) | (block_of(source) == far), factor * values, values)


def shard_levels(stream_key, dims, split, low, top_value):
    gain, own = 1.0, jax.random.fold_in(stream_key, 6)
    for dim, parts in split:
        steps = jnp.exp(jax.random.uniform(jax.random.fold_in(own, dim), (parts,), jnp.float32, low / len(split), top_value / len(split)))
        gain = gain * jnp.repeat(steps, dims[dim] // parts).reshape([-1 if axis == dim else 1 for axis in range(len(dims))])
    return gain


def normal_values(stream_key, shape, spread, reach, cuts=(), kind=jnp.bfloat16):
    array = spread * jax.random.normal(stream_key, shape, jnp.float32)
    if cuts:
        array = array * shard_levels(stream_key, shape, cuts, -0.22, 0.18)
    return jnp.clip(array, -reach, reach).astype(kind)


def noise_with(stream_key, shape, spread, bound, pieces, heavy, dtype=jnp.bfloat16):
    array = spread * jax.random.normal(stream_key, shape, jnp.float32)
    if pieces:
        array = array * shard_levels(stream_key, shape, pieces, -0.22, 0.18)
    return jnp.clip(raised(array, jax.random.fold_in(stream_key, 3), *heavy), -bound, bound).astype(dtype)


def setup_inputs(seed: int = 0) -> dict:
    key_list = jax.random.split(jax.random.key(seed), 8)
    partials = noise_with(key_list[0], (N_DP, BLOCKS, BLK, BLK), 0.2, 6.0, ((0, 32), (1, 16)), (0, 2, 32, 2.75))
    params = normal_values(key_list[1], (BLOCKS, BLK, BLK), 0.05, 0.75, ((0, 16), (1, 32)), jnp.float32)
    left_basis = normal_values(key_list[2], (N_DP, N_SHARD, CAP, BLK, BLK), BLK ** -0.5, 0.375, ((0, 32), (1, 16)), jnp.float32)
    right_basis = normal_values(key_list[3], (N_DP, N_SHARD, CAP, BLK, BLK), BLK ** -0.5, 0.375, ((0, 32), (1, 16)), jnp.float32)
    first_moment = normal_values(key_list[4], (N_DP, N_SHARD, CAP, BLK, BLK), 0.3, 4.0, ((0, 32), (1, 16)), jnp.float32)
    second_moment = jnp.clip(jnp.exp(math.log(10.0) - 4.6051702 * jax.random.uniform(key_list[5], (N_DP, N_SHARD, CAP, BLK, BLK), jnp.float32) ** shard_levels(key_list[5], (N_DP, N_SHARD, CAP, BLK, BLK), ((0, 32), (1, 16)), -0.2, 0.2)), 0.1, 10.0)
    owner_list = draw_owner_list(jax.random.fold_in(key_list[7], 71), 0)
    return {"partials": partials, "params": params, "left_basis": left_basis, "right_basis": right_basis, "first_moment": first_moment, "second_moment": second_moment, "owner_list": owner_list}


beta_one = 0.9
beta_two = 0.95
epsilon = 1e-08
learn_rate = 0.2
decay_rate = 0.1
step_count = 10

def reference(partials, params, left_basis, right_basis, first_moment, second_moment, owner_list):
    highest = lax.Precision.HIGHEST
    gradient = lax.optimization_barrier(jnp.sum(partials.astype(jnp.float32), axis=0))
    first_out = first_moment
    second_out = second_moment
    correct_one = 1.0 - beta_one ** step_count
    correct_two = 1.0 - beta_two ** step_count
    updated_list = []
    for block_index in range(BLOCKS):
        owner_idx = owner_list[block_index]
        owner_row = (owner_idx // N_SHARD).astype(jnp.int32)
        owner_col = (owner_idx % N_SHARD).astype(jnp.int32)
        left_mat = left_basis[owner_row, owner_col, 0]
        right_mat = right_basis[owner_row, owner_col, 0]
        first_old = first_moment[owner_row, owner_col, 0]
        second_old = second_moment[owner_row, owner_col, 0]
        partway = jnp.dot(left_mat.T, gradient[block_index], precision=highest, preferred_element_type=jnp.float32)
        rotated = jnp.dot(partway, right_mat, precision=highest, preferred_element_type=jnp.float32)
        first_new = beta_one * first_old + (1.0 - beta_one) * rotated
        second_new = beta_two * second_old + (1.0 - beta_two) * rotated * rotated
        scaled = first_new / correct_one / (jnp.sqrt(second_new / correct_two) + epsilon)
        back_rot = jnp.dot(scaled, right_mat.T, precision=highest, preferred_element_type=jnp.float32)
        change = jnp.dot(left_mat, back_rot, precision=highest, preferred_element_type=jnp.float32)
        updated_list.append(params[block_index] - learn_rate * (change + decay_rate * params[block_index]))
        first_out = first_out.at[owner_row, owner_col, 0].set(first_new)
        second_out = second_out.at[owner_row, owner_col, 0].set(second_new)
    return (jnp.stack(updated_list), first_out, second_out)
```

```python
import functools

import jax
import jax.numpy as jnp
from jax import lax
from jax.experimental import pallas as pl
from jax.experimental.pallas import tpu as pltpu
from jax.sharding import PartitionSpec as P

beta_one = 0.9
beta_two = 0.95
epsilon = 1e-08
learn_rate = 0.2
decay_rate = 0.1
step_count = 10

MESH = pl.DeviceIdType.MESH
F32 = jnp.float32
BF16 = jnp.bfloat16
NX, NY, NZ, NC = 4, 8, 8, 2
ND, NS = NX * NY, NZ * NC
HALVES = (0, 1)


def split(value):
    high = value.astype(BF16)
    return high, (value - high.astype(F32)).astype(BF16)


def dot(left, right):
    return jnp.dot(left, right, preferred_element_type=F32)


def dot3(left, right):
    return dot(left[0], right[0]) + (dot(left[0], right[1]) + dot(left[1], right[0]))


def body(
    own_hbm, part_hbm, params_hbm, left_hbm, right_hbm, first_hbm, second_hbm,
    out_hbm, first_out_hbm, second_out_hbm,
    own_vec, own_ref, idx_vec, idx_ref, part, params, left, right, first, second, first_new, second_new,
    acc_x, acc_y, in_x, in_y, small_x, small_y,
    every_0, every_1, chosen, whole, change, coming_0, coming_1, sib_out, sib_in, mine, z_in, fresh,
    l_hi, l_lo, lt_hi, lt_lo, r_hi, r_lo, rt_hi, rt_lo,
    meter, load_sem, idx_sem, send_sem, x_sem, y_sem, sx_sem, sy_sem, z_sem, zs_sem, c_sem, e_sem, fs_sem, f_sem,
    gsy_sem, gsx_sem, gx_sem, gy_sem, keep_sem, out_sem,
):
    d = lax.axis_index("dp")
    s = lax.axis_index("shard")
    y, x = lax.div(d, NX), lax.rem(d, NX)
    z, c = lax.div(s, NC), lax.rem(s, NC)
    f = 1 - 2 * c

    def xs(k):
        return lax.rem(x + k + 2 * NX, NX)

    def ys(k):
        return lax.rem(y + k + 2 * NY, NY)

    def zs(k):
        return lax.rem(z + k + NZ, NZ)

    def at_x(k):
        return (y * NX + xs(k), s)

    def at_y(k):
        return (ys(k) * NX + x, s)

    def at_z(k):
        return (d, zs(k) * NC + c)

    def at_d(k):
        return lax.rem(d + k, ND)

    sibling = (d, z * NC + 1 - c)
    every = (every_0, every_1)
    coming = (coming_0, coming_1)
    sent = [0]
    stores = []

    def send(src, dst, recv, device, tiles):
        copy = pltpu.make_async_remote_copy(
            src_ref=src, dst_ref=dst, send_sem=send_sem.at[0], recv_sem=recv, device_id=device, device_id_type=MESH
        )
        copy.start()
        sent[0] += tiles

    def arrived(ref, sem):
        pltpu.make_async_copy(ref, ref, sem).wait()

    def block_at(slot_index):
        return jnp.maximum(idx_ref[slot_index, 0] - 1, 0)

    def finish():
        arrived(meter.at[pl.ds(0, sent[0])], send_sem.at[0])
        for store in stores:
            store.wait()

    def out_x(h, xi, yi):
        return out_hbm.at[pl.ds(0, 4), yi, xi, :, pl.ds(128 * h, 128)]

    def out_y(h, yi, xi):
        return out_hbm.at[pl.ds(4, 4), yi, xi, :, pl.ds(128 * h, 128)]

    def all_x(h, xi):
        return out_hbm.at[pl.ds(0, 4), :, xi, :, pl.ds(128 * h, 128)]

    def all_y(h, yi):
        return out_hbm.at[pl.ds(4, 4), yi, :, :, pl.ds(128 * h, 128)]

    def in_order(*streams):
        waiting = [(0.0, place, stream) for place, stream in enumerate(streams)]
        while waiting:
            waiting.sort(key=lambda entry: entry[:2])
            _, place, stream = waiting.pop(0)
            time = next(stream, None)
            if time is not None:
                waiting.append((time, place, stream))

    loads = [
        pltpu.make_async_copy(src, dst, load_sem.at[i])
        for i, (src, dst) in enumerate(
            (
                (own_hbm, own_vec), (part_hbm.at[pl.ds(4, 4)], part.at[pl.ds(4, 4)]),
                (part_hbm.at[pl.ds(0, 4)], part.at[pl.ds(0, 4)]),
                (left_hbm, left), (right_hbm, right), (first_hbm, first), (second_hbm, second), (params_hbm, params), (own_hbm, own_ref),
            )
        )
    ]
    for load in loads:
        load.start()

    barrier = pltpu.get_barrier_semaphore()
    for k in range(1, ND):
        pl.semaphore_signal(barrier, inc=1, device_id=(at_d(k), s), device_id_type=MESH)
    for k in range(1, NZ):
        pl.semaphore_signal(barrier, inc=1, device_id=at_z(k), device_id_type=MESH)
    pl.semaphore_signal(barrier, inc=1, device_id=sibling, device_id_type=MESH)

    loads[0].wait()
    block = lax.broadcasted_iota(jnp.int32, (ND, 128), 1)
    home, inner = lax.div(block, 8), lax.rem(block, 8)
    place = ((lax.div(inner, 4) * NC + lax.rem(home, NC)) * NZ + lax.div(home, NC)) * 4 + lax.rem(inner, 4) + 1
    slot = lax.broadcasted_iota(jnp.int32, (ND, 128), 0) * NS + s
    found = jnp.max(jnp.where(own_vec[...] == slot, place, 0), axis=1, keepdims=True)
    idx_vec[...] = jnp.broadcast_to(found, (ND, 128))
    idx_copy = pltpu.make_async_copy(idx_vec, idx_ref, idx_sem.at[0])
    idx_copy.start()

    loads[1].wait()

    @pl.loop(0, 4)
    def _(blk):
        for yi in range(NY):
            rows = part[4 + blk, 32 * yi : 32 * yi + 32, :].astype(F32)
            for xi in range(NX):
                for h in HALVES:
                    acc_y[h, yi, blk, xi] = rows[8 * xi : 8 * xi + 8, 128 * h : 128 * h + 128]

    loads[2].wait()

    @pl.loop(0, 4)
    def _(blk):
        for yi in range(NY):
            rows = part[blk, 32 * yi : 32 * yi + 32, :].astype(F32)
            for xi in range(NX):
                for h in HALVES:
                    acc_x[h, xi, blk, yi] = rows[8 * xi : 8 * xi + 8, 128 * h : 128 * h + 128]

    pl.semaphore_wait(barrier, ND - 1 + NZ - 1 + 1)

    def spread(kind, h, total):
        own = every[h].at[kind, c, z]
        every[h][kind, c, z] = total
        for k in range(1, NZ):
            send(own, own, z_sem.at[h, kind, k - 1], at_z(k), 4)
        send(own, own, zs_sem.at[h, kind], sibling, 4)

    def relay(kind, h):
        for k in (1, 7, 2, 6, 3, 5, 4):
            chunk = every[h].at[kind, c, zs(-k)]
            arrived(chunk, z_sem.at[h, kind, k - 1])
            send(chunk, chunk, zs_sem.at[h, kind], sibling, 4)

    def x_unit(h):
        send(acc_x.at[h, xs(2)], in_x.at[h, 0], x_sem.at[h, 0], at_x(f), 32)
        send(acc_x.at[h, xs(-f)], in_x.at[h, 2], x_sem.at[h, 2], at_x(-f), 32)
        yield 4.4 + 2.5 * h
        arrived(in_x.at[h, 0], x_sem.at[h, 0])
        acc_x[h, xs(f)] += in_x[h, 0]
        send(acc_x.at[h, xs(f)], in_x.at[h, 1], x_sem.at[h, 1], at_x(f), 32)
        yield 8.2 + 1.3 * h
        arrived(in_x.at[h, 2], x_sem.at[h, 2])
        arrived(in_x.at[h, 1], x_sem.at[h, 1])
        acc_x[h, x] += in_x[h, 1] + in_x[h, 2]
        for k in range(1, NY):
            send(acc_x.at[h, x, :, ys(k)], small_y.at[h, k - 1], sy_sem.at[h], at_y(k), 4)
        yield 12.5 + 2.0 * h
        arrived(small_y.at[h], sy_sem.at[h])
        total = acc_x[h, x, :, y]
        for k in range(NY - 1):
            total += small_y[h, k]
        spread(0, h, total)
        yield 17.0 + 3.0 * h
        relay(0, h)

    def y_unit(h):
        send(acc_y.at[h, ys(4)], in_y.at[h, 0], y_sem.at[h, 0], at_y(f), 16)
        send(acc_y.at[h, ys(-3 * f)], in_y.at[h, 4], y_sem.at[h, 4], at_y(-f), 16)
        for step in range(3):
            yield 3.0 * (step + 1) + 1.3 * h
            arrived(in_y.at[h, step], y_sem.at[h, step])
            far = ys((3 - step) * f)
            acc_y[h, far] += in_y[h, step]
            send(acc_y.at[h, far], in_y.at[h, step + 1], y_sem.at[h, step + 1], at_y(f), 16)
            if step < 2:
                arrived(in_y.at[h, 4 + step], y_sem.at[h, 4 + step])
                far = ys(-(2 - step) * f)
                acc_y[h, far] += in_y[h, 4 + step]
                send(acc_y.at[h, far], in_y.at[h, 5 + step], y_sem.at[h, 5 + step], at_y(-f), 16)
        yield 12.0 + 1.3 * h
        arrived(in_y.at[h, 3], y_sem.at[h, 3])
        arrived(in_y.at[h, 6], y_sem.at[h, 6])
        acc_y[h, y] += in_y[h, 3] + in_y[h, 6]
        for k in range(1, NX):
            send(acc_y.at[h, y, :, xs(k)], small_x.at[h, k - 1], sx_sem.at[h], at_x(k), 4)
        yield 14.5 + 1.3 * h
        arrived(small_x.at[h], sx_sem.at[h])
        total = acc_y[h, y, :, x]
        for k in range(NX - 1):
            total += small_x[h, k]
        spread(1, h, total)
        yield 19.0 + 3.0 * h
        relay(1, h)

    def bases():
        yield 2.0
        for load in loads[3:]:
            load.wait()
        idx_copy.wait()
        value = left[...]
        l_hi[...], l_lo[...] = split(value)
        yield 2.1
        lt_hi[...], lt_lo[...] = split(left[...].T)
        yield 5.0
        value = right[...]
        r_hi[...], r_lo[...] = split(value)
        yield 8.0
        rt_hi[...], rt_lo[...] = split(right[...].T)

    def to_owners(h):
        yield 21.0 + 3.0 * h
        for kind in range(2):
            arrived(every[h].at[kind, 1 - c], zs_sem.at[h, kind])
        flat = every[h].reshape(128, 8, 128)
        whole[h, d] = flat[block_at(d)]
        for k in range(1, ND):
            to = at_d(k)
            chosen[h, to] = flat[block_at(to)]
            send(chosen.at[h, to], whole.at[h, d], c_sem.at[h], (to, s), 1)

    in_order(y_unit(0), x_unit(0), y_unit(1), x_unit(1), bases(), to_owners(0), to_owners(1))

    partway = []
    for h in HALVES:
        arrived(whole.at[h, pl.ds(0, ND - 1)], c_sem.at[h])
        partway.append(dot3((lt_hi[...], lt_lo[...]), split(whole[h].reshape(256, 128))))
    rotated = dot3(split(partway[0]), (r_hi[0:128], r_lo[0:128])) + dot3(
        split(partway[1]), (r_hi[128:256], r_lo[128:256])
    )
    first_old, second_old = first[...], second[...]
    first_val = beta_one * first_old + (1.0 - beta_one) * rotated
    second_val = beta_two * second_old + (1.0 - beta_two) * rotated * rotated
    correct_one = 1.0 - beta_one**step_count
    correct_two = 1.0 - beta_two**step_count
    scaled = split(first_val / correct_one / (jnp.sqrt(second_val / correct_two) + epsilon))
    for h in HALVES:
        back = dot3(scaled, (rt_hi[:, 128 * h : 128 * h + 128], rt_lo[:, 128 * h : 128 * h + 128]))
        change[h] = dot3((l_hi[...], l_lo[...]), split(back)).reshape(ND, 8, 128)
        coming[h][d] = change[h, d]
        for k in range(1, ND):
            to = at_d(k)
            send(change.at[h, to], coming[h].at[d], e_sem.at[h], (to, s), 1)
    live = idx_ref[d, 0] > 0
    first_new[...] = jnp.where(live, first_val, first_old)
    second_new[...] = jnp.where(live, second_val, second_old)
    stores.append(pltpu.make_async_copy(first_new, first_out_hbm, out_sem.at[0]))
    stores.append(pltpu.make_async_copy(second_new, second_out_hbm, out_sem.at[1]))
    for store in stores:
        store.start()

    def rows_of(kind, h, zi, core, blk):
        who = own_ref[0, (zi * NC + core) * 8 + 4 * kind + blk]
        return jnp.where((who & (NS - 1)) == s, coming[h][who >> 4], 0.0)

    def gather_sibling(kind, h):
        for zi in range(NZ):
            for blk in range(4):
                sib_out[h, kind, zi, blk] = rows_of(kind, h, zi, 1 - c, blk)
        send(sib_out.at[h, kind], sib_in.at[h, kind], fs_sem.at[h, kind], sibling, 32)

    def gather_mine(kind, h):
        for zi in range(NZ):
            for blk in range(4):
                mine[h, kind, zi, blk] = rows_of(kind, h, zi, c, blk)

    def home_sends(kind, h):
        arrived(sib_in.at[h, kind], fs_sem.at[h, kind])
        for k in range(1, NZ):
            mine[h, kind, zs(k)] += sib_in[h, kind, zs(k)]
            send(mine.at[h, kind, zs(k)], z_in.at[h, kind, k - 1], f_sem.at[h, kind], at_z(k), 4)

    def home_rows(kind, h):
        arrived(z_in.at[h, kind], f_sem.at[h, kind])
        total = mine[h, kind, z] + sib_in[h, kind, z]
        for k in range(NZ - 1):
            total += z_in[h, kind, k]
        old = params[4 * kind : 4 * kind + 4, :, 128 * h : 128 * h + 128]
        fresh[h, kind] = old - learn_rate * (total + decay_rate * old)

    def y_back(h):
        yield 0.0 + 2.0 * h
        arrived(coming[h].at[pl.ds(0, ND - 1)], e_sem.at[h])
        gather_sibling(1, h)
        gather_sibling(0, h)
        gather_mine(1, h)
        yield 1.5 + 2.0 * h
        home_sends(1, h)
        yield 6.5 + 2.0 * h
        home_rows(1, h)
        pltpu.make_async_copy(fresh.at[h, 1], out_y(h, y, x), keep_sem.at[h, 1]).start()
        for k in range(1, NX):
            send(fresh.at[h, 1], out_y(h, y, x), gsx_sem.at[h], at_x(k), 4)
        yield 9.0 + 2.0 * h
        arrived(fresh.at[h, 1], keep_sem.at[h, 1])
        arrived(all_y(h, 0).at[:, pl.ds(0, NX - 1)], gsx_sem.at[h])
        send(all_y(h, y), all_y(h, y), gy_sem.at[h, 0], at_y(f), 16)
        send(all_y(h, y), all_y(h, y), gy_sem.at[h, 4], at_y(-f), 16)
        for step in range(4):
            yield 12.0 + 3.0 * step + 1.5 * h
            chunk = all_y(h, ys(-(step + 1) * f))
            arrived(chunk, gy_sem.at[h, step])
            if step < 3:
                send(chunk, chunk, gy_sem.at[h, step + 1], at_y(f), 16)
                chunk = all_y(h, ys((step + 1) * f))
                arrived(chunk, gy_sem.at[h, 4 + step])
                if step < 2:
                    send(chunk, chunk, gy_sem.at[h, 5 + step], at_y(-f), 16)

    def x_back(h):
        yield 4.0 + 1.0 * h
        gather_mine(0, h)
        home_sends(0, h)
        yield 10.0 + 2.0 * h
        home_rows(0, h)
        pltpu.make_async_copy(fresh.at[h, 0], out_x(h, x, y), keep_sem.at[h, 0]).start()
        for k in range(1, NY):
            send(fresh.at[h, 0], out_x(h, x, y), gsy_sem.at[h], at_y(k), 4)
        yield 14.0 + 2.0 * h
        arrived(fresh.at[h, 0], keep_sem.at[h, 0])
        arrived(all_x(h, 0).at[:, pl.ds(0, NY - 1)], gsy_sem.at[h])
        send(all_x(h, x), all_x(h, x), gx_sem.at[h, 0], at_x(f), 32)
        send(all_x(h, x), all_x(h, x), gx_sem.at[h, 2], at_x(-f), 32)
        yield 18.0 + 2.5 * h
        chunk = all_x(h, xs(-f))
        arrived(chunk, gx_sem.at[h, 0])
        send(chunk, chunk, gx_sem.at[h, 1], at_x(f), 32)
        yield 23.0 + 2.5 * h
        arrived(all_x(h, xs(f)), gx_sem.at[h, 2])
        arrived(all_x(h, xs(2)), gx_sem.at[h, 1])

    in_order(y_back(0), y_back(1), x_back(0), x_back(1))
    finish()


def local(partials, params, left_basis, right_basis, first_moment, second_moment, owner_list):
    dma = pltpu.SemaphoreType.DMA
    full = (256, 256)
    vm = pltpu.VMEM
    any_spec = pl.BlockSpec(memory_space=pl.ANY)
    in_hbm = functools.partial(pltpu.with_memory_space_constraint, memory_space=pltpu.HBM)
    updated, first_out, second_out = pl.pallas_call(
        body,
        out_shape=(
            pltpu.VMEM((8, NY, NX, 8, 256), F32),
            pltpu.VMEM(full, F32),
            pltpu.VMEM(full, F32),
        ),
        in_specs=[any_spec] * 7,
        out_specs=(any_spec,) * 3,
        scratch_shapes=[
            vm((1, 128), jnp.int32), pltpu.SMEM((1, 128), jnp.int32), vm((ND, 128), jnp.int32), pltpu.SMEM((ND, 128), jnp.int32),
            vm((8, 256, 256), BF16), vm((8, 8, 256), F32),
            vm(full, F32), vm(full, F32), vm(full, F32), vm(full, F32), vm(full, F32), vm(full, F32),
            vm((2, NX, 4, NY, 8, 128), F32), vm((2, NY, 4, NX, 8, 128), F32),
            vm((2, 3, 4, NY, 8, 128), F32), vm((2, 7, 4, NX, 8, 128), F32),
            vm((2, NX - 1, 4, 8, 128), F32), vm((2, NY - 1, 4, 8, 128), F32),
            vm((2, NC, NZ, 4, 8, 128), F32), vm((2, NC, NZ, 4, 8, 128), F32),
            vm((2, ND, 8, 128), F32), vm((2, ND, 8, 128), F32),
            vm((2, ND, 8, 128), F32), vm((ND, 8, 128), F32), vm((ND, 8, 128), F32),
            vm((2, 2, NZ, 4, 8, 128), F32), vm((2, 2, NZ, 4, 8, 128), F32), vm((2, 2, NZ, 4, 8, 128), F32),
            vm((2, 2, NZ - 1, 4, 8, 128), F32), vm((2, 2, 4, 8, 128), F32),
            vm(full, BF16), vm(full, BF16), vm(full, BF16), vm(full, BF16),
            vm(full, BF16), vm(full, BF16), vm(full, BF16), vm(full, BF16),
            vm((3072, 8, 128), F32),
            dma((9,)), dma((1,)), dma((1,)), dma((2, 3)), dma((2, 7)), dma((2,)), dma((2,)), dma((2, 2, 7)), dma((2, 2)),
            dma((2,)), dma((2,)), dma((2, 2)), dma((2, 2)), dma((2,)), dma((2,)), dma((2, 3)), dma((2, 7)), dma((2, 2)),
            dma((2,)),
        ],
        compiler_params=pltpu.CompilerParams(
            collective_id=0, has_side_effects=True, vmem_limit_bytes=48 * 1024 * 1024
        ),
        name="soap_step",
    )(
        *map(
            in_hbm,
            (
                owner_list.reshape(1, 128), partials[0], params, left_basis[0, 0, 0], right_basis[0, 0, 0],
                first_moment[0, 0, 0], second_moment[0, 0, 0],
            ),
        )
    )
    return (
        updated.reshape(8, 256, 256),
        first_out[None, None, None],
        second_out[None, None, None],
    )


def solution(mesh):
    return jax.shard_map(
        local,
        mesh=mesh,
        in_specs=(
            P("dp", "shard", None, None),
            P("shard", "dp", None),
            P("dp", "shard", None, None, None),
            P("dp", "shard", None, None, None),
            P("dp", "shard", None, None, None),
            P("dp", "shard", None, None, None),
            P(),
        ),
        out_specs=(
            P("shard", None, None),
            P("dp", "shard", None, None, None),
            P("dp", "shard", None, None, None),
        ),
        check_vma=False,
    )
```

```python
import functools

import jax
import jax.numpy as jnp
from jax import lax
from jax.experimental import pallas as pl
from jax.experimental.pallas import tpu as pltpu
from jax.sharding import PartitionSpec as P

beta_one = 0.9
beta_two = 0.95
epsilon = 1e-08
learn_rate = 0.2
decay_rate = 0.1
step_count = 10

MESH = pl.DeviceIdType.MESH
F32 = jnp.float32
BF16 = jnp.bfloat16
NX, NY, NZ, NC = 4, 8, 8, 2
ND, NS = NX * NY, NZ * NC
HALVES = (0, 1)

TIMES = {
    "x0": (5, 3),
    "x1": (9, 3),
    "x2": (14, 3),
    "x3": (17.1, 3.0),
    "x4": (20.6, 3.0),
    "y0": (3, 1.5),
    "y1": (6, 1.5),
    "y2": (9, 1.5),
    "y3": (12, 2),
    "y4": (14.2, 2.2),
    "y5": (17, 3.0),
    "y6": (20.5, 3.0),
    "c": (20.7, 3.0),
    "b0": (0, 2),
    "b00": (1.5, 2),
    "b1": (1.6, 2),
    "b2": (4.5, 2),
    "b3": (7.5, 2),
    "b4": (10.5, 2),
    "g0": (14.5, 1.5),
    "g1": (17.5, 1.5),
    "g2": (20.5, 1.5),
    "g3": (23.5, 1.5),
    "a0": (2.0, 2),
    "a1": (5.0, 2),
    "a2": (8.0, 2),
    "a3": (13, 2),
    "a4": (17.5, 2.5),
    "a5": (22, 2.5),
}


def at(step, half):
    start, later = TIMES[step]
    return start + later * half


def split(value):
    high = value.astype(BF16)
    return high, (value - high.astype(F32)).astype(BF16)


def dot(left, right):
    return jnp.dot(left, right, preferred_element_type=F32)


def dot3(left, right):
    return dot(left[0], right[0]) + (dot(left[0], right[1]) + dot(left[1], right[0]))


def body(
    own_hbm, part_hbm, params_hbm, left_hbm, right_hbm, first_hbm, second_hbm,
    out_hbm, first_out_hbm, second_out_hbm,
    own_vec, own_ref, idx_vec, idx_ref, part, params, left, right, first, second, first_new, second_new,
    acc_x, acc_y, in_x, in_y, small_x, small_y,
    every_0, every_1, chosen, whole, change, coming_0, coming_1, mine, z_in, fresh,
    l_hi, l_lo, lt_hi, lt_lo, r_hi, r_lo, rt_hi, rt_lo,
    meter, load_sem, idx_sem, send_sem, x_sem, y_sem, sx_sem, sy_sem, z_sem, zs_sem, c_sem, e_sem, fs_sem, f_sem,
    gsy_sem, gsx_sem, gx_sem, gy_sem, keep_sem, out_sem,
):
    d = lax.axis_index("dp")
    s = lax.axis_index("shard")
    y, x = lax.div(d, NX), lax.rem(d, NX)
    z, c = lax.div(s, NC), lax.rem(s, NC)
    f = 1 - 2 * c

    def xs(k):
        return lax.rem(x + k + 2 * NX, NX)

    def ys(k):
        return lax.rem(y + k + 2 * NY, NY)

    def zs(k):
        return lax.rem(z + k + NZ, NZ)

    def at_x(k):
        return (y * NX + xs(k), s)

    def at_y(k):
        return (ys(k) * NX + x, s)

    def at_z(k):
        return (d, zs(k) * NC + c)

    def at_d(k):
        return lax.rem(d + k, ND)

    others = [
        ys(j) * NX + xs(i)
        for j, i in sorted(
            ((j, i) for j in range(NY) for i in range(NX) if j or i),
            key=lambda to: -min(to[0], NY - to[0]) - min(to[1], NX - to[1]),
        )
    ]

    sibling = (d, z * NC + 1 - c)
    every = (every_0, every_1)
    coming = (coming_0, coming_1)
    sent = [0]
    stores = []

    def send(src, dst, recv, device, tiles):
        copy = pltpu.make_async_remote_copy(
            src_ref=src, dst_ref=dst, send_sem=send_sem.at[0], recv_sem=recv, device_id=device, device_id_type=MESH
        )
        copy.start()
        sent[0] += tiles

    def arrived(ref, sem):
        pltpu.make_async_copy(ref, ref, sem).wait()

    def block_at(slot_index):
        return jnp.maximum(idx_ref[slot_index, 0] - 1, 0)

    def finish():
        arrived(meter.at[pl.ds(0, sent[0])], send_sem.at[0])
        for store in stores:
            store.wait()

    def out_x(h, xi, yi):
        return out_hbm.at[pl.ds(0, 4), yi, xi, :, pl.ds(128 * h, 128)]

    def out_y(h, yi, xi):
        return out_hbm.at[pl.ds(4, 4), yi, xi, :, pl.ds(128 * h, 128)]

    def all_x(h, xi):
        return out_hbm.at[pl.ds(0, 4), :, xi, :, pl.ds(128 * h, 128)]

    def all_y(h, yi):
        return out_hbm.at[pl.ds(4, 4), yi, :, :, pl.ds(128 * h, 128)]

    def in_order(*streams):
        waiting = [(0.0, place, stream) for place, stream in enumerate(streams)]
        while waiting:
            waiting.sort(key=lambda entry: entry[:2])
            _, place, stream = waiting.pop(0)
            time = next(stream, None)
            if time is not None:
                waiting.append((time, place, stream))

    loads = [
        pltpu.make_async_copy(src, dst, load_sem.at[i])
        for i, (src, dst) in enumerate(
            (
                (own_hbm, own_vec), (part_hbm.at[pl.ds(4, 4)], part.at[pl.ds(4, 4)]),
                (part_hbm.at[pl.ds(0, 4)], part.at[pl.ds(0, 4)]),
                (left_hbm, left), (right_hbm, right), (first_hbm, first), (second_hbm, second), (params_hbm, params), (own_hbm, own_ref),
            )
        )
    ]
    for load in loads:
        load.start()

    barrier = pltpu.get_barrier_semaphore()
    for k in range(1, ND):
        pl.semaphore_signal(barrier, inc=1, device_id=(at_d(k), s), device_id_type=MESH)
    for k in range(1, NZ):
        pl.semaphore_signal(barrier, inc=1, device_id=at_z(k), device_id_type=MESH)
    pl.semaphore_signal(barrier, inc=1, device_id=sibling, device_id_type=MESH)

    loads[1].wait()

    @pl.loop(0, 4)
    def _(blk):
        for yi in range(NY):
            rows = part[4 + blk, 32 * yi : 32 * yi + 32, :].astype(F32)
            for xi in range(NX):
                for h in HALVES:
                    acc_y[h, yi, blk, xi] = rows[8 * xi : 8 * xi + 8, 128 * h : 128 * h + 128]

    loads[2].wait()

    @pl.loop(0, 4)
    def _(blk):
        for yi in range(NY):
            rows = part[blk, 32 * yi : 32 * yi + 32, :].astype(F32)
            for xi in range(NX):
                for h in HALVES:
                    acc_x[h, xi, blk, yi] = rows[8 * xi : 8 * xi + 8, 128 * h : 128 * h + 128]

    pl.semaphore_wait(barrier, ND - 1 + NZ - 1 + 1)

    def spread(kind, h, total):
        own = every[h].at[kind, c, z]
        every[h][kind, c, z] = total
        for k, i in ((2, 0), (-2, 1), (1, 2), (-1, 3)):
            send(own, own, z_sem.at[h, kind, i], at_z(k * f), 4)
        send(own, own, zs_sem.at[h, kind], sibling, 4)

    def relay(kind, h):
        for k, i, onward in ((-2, 0, ((2, 6), (1, 4))), (2, 1, ((-1, 5),)), (-1, 2, ()), (1, 3, ())):
            chunk = every[h].at[kind, c, zs(k * f)]
            arrived(chunk, z_sem.at[h, kind, i])
            for via, j in onward:
                send(chunk, chunk, z_sem.at[h, kind, j], at_z(via * f), 4)
            send(chunk, chunk, zs_sem.at[h, kind], sibling, 4)

    def relay_far(kind, h):
        for k, i in ((-3, 4), (3, 5), (4, 6)):
            chunk = every[h].at[kind, c, zs(k * f)]
            arrived(chunk, z_sem.at[h, kind, i])
            send(chunk, chunk, zs_sem.at[h, kind], sibling, 4)

    def x_unit(h):
        send(acc_x.at[h, xs(2)], in_x.at[h, 0], x_sem.at[h, 0], at_x(f), 32)
        send(acc_x.at[h, xs(-f)], in_x.at[h, 2], x_sem.at[h, 2], at_x(-f), 32)
        yield at("x0", h)
        arrived(in_x.at[h, 0], x_sem.at[h, 0])
        acc_x[h, xs(f)] += in_x[h, 0]
        send(acc_x.at[h, xs(f)], in_x.at[h, 1], x_sem.at[h, 1], at_x(f), 32)
        yield at("x1", h)
        arrived(in_x.at[h, 2], x_sem.at[h, 2])
        arrived(in_x.at[h, 1], x_sem.at[h, 1])
        acc_x[h, x] += in_x[h, 1] + in_x[h, 2]
        for k in (4, 3, 5, 2, 6, 1, 7):
            send(acc_x.at[h, x, :, ys(k)], small_y.at[h, k - 1], sy_sem.at[h], at_y(k), 4)
        yield at("x2", h)
        arrived(small_y.at[h], sy_sem.at[h])
        total = acc_x[h, x, :, y]
        for k in range(NY - 1):
            total += small_y[h, k]
        spread(0, h, total)
        yield at("x3", h)
        relay(0, h)
        yield at("x4", h)
        relay_far(0, h)

    def y_unit(h):
        send(acc_y.at[h, ys(4)], in_y.at[h, 0], y_sem.at[h, 0], at_y(f), 16)
        send(acc_y.at[h, ys(-3 * f)], in_y.at[h, 4], y_sem.at[h, 4], at_y(-f), 16)
        for step in range(3):
            yield at(f"y{step}", h)
            arrived(in_y.at[h, step], y_sem.at[h, step])
            far = ys((3 - step) * f)
            acc_y[h, far] += in_y[h, step]
            send(acc_y.at[h, far], in_y.at[h, step + 1], y_sem.at[h, step + 1], at_y(f), 16)
            if step < 2:
                arrived(in_y.at[h, 4 + step], y_sem.at[h, 4 + step])
                far = ys(-(2 - step) * f)
                acc_y[h, far] += in_y[h, 4 + step]
                send(acc_y.at[h, far], in_y.at[h, 5 + step], y_sem.at[h, 5 + step], at_y(-f), 16)
        yield at("y3", h)
        arrived(in_y.at[h, 3], y_sem.at[h, 3])
        arrived(in_y.at[h, 6], y_sem.at[h, 6])
        acc_y[h, y] += in_y[h, 3] + in_y[h, 6]
        for k in (2, 1, 3):
            send(acc_y.at[h, y, :, xs(k)], small_x.at[h, k - 1], sx_sem.at[h], at_x(k), 4)
        yield at("y4", h)
        arrived(small_x.at[h], sx_sem.at[h])
        total = acc_y[h, y, :, x]
        for k in range(NX - 1):
            total += small_x[h, k]
        spread(1, h, total)
        yield at("y5", h)
        relay(1, h)
        yield at("y6", h)
        relay_far(1, h)

    def bases():
        yield 2.0
        loads[0].wait()
        block = lax.broadcasted_iota(jnp.int32, (ND, 128), 1)
        home, inner = lax.div(block, 8), lax.rem(block, 8)
        place = ((lax.div(inner, 4) * NC + lax.rem(home, NC)) * NZ + lax.div(home, NC)) * 4 + lax.rem(inner, 4) + 1
        slot = lax.broadcasted_iota(jnp.int32, (ND, 128), 0) * NS + s
        found = jnp.max(jnp.where(own_vec[...] == slot, place, 0), axis=1, keepdims=True)
        idx_vec[...] = jnp.broadcast_to(found, (ND, 128))
        idx_copy = pltpu.make_async_copy(idx_vec, idx_ref, idx_sem.at[0])
        idx_copy.start()
        for load in loads[3:]:
            load.wait()
        value = left[...]
        l_hi[...], l_lo[...] = split(value)
        yield 2.1
        lt_hi[...], lt_lo[...] = split(left[...].T)
        yield 5.0
        value = right[...]
        r_hi[...], r_lo[...] = split(value)
        yield 8.0
        rt_hi[...], rt_lo[...] = split(right[...].T)
        idx_copy.wait()

    def to_owners(h):
        yield at("c", h)
        for kind in range(2):
            arrived(every[h].at[kind, 1 - c], zs_sem.at[h, kind])
        flat = every[h].reshape(128, 8, 128)
        whole[h, d] = flat[block_at(d)]
        for to in others:
            chosen[h, to] = flat[block_at(to)]
            send(chosen.at[h, to], whole.at[h, d], c_sem.at[h], (to, s), 1)

    in_order(y_unit(0), x_unit(0), y_unit(1), x_unit(1), bases(), to_owners(0), to_owners(1))

    rotated = 0.0
    for h in HALVES:
        arrived(whole.at[h, pl.ds(0, ND - 1)], c_sem.at[h])
        partway = dot3((lt_hi[...], lt_lo[...]), split(whole[h].reshape(256, 128)))
        rows = slice(128 * h, 128 * h + 128)
        rotated += dot3(split(partway), (r_hi[rows], r_lo[rows]))
    first_old, second_old = first[...], second[...]
    first_val = beta_one * first_old + (1.0 - beta_one) * rotated
    second_val = beta_two * second_old + (1.0 - beta_two) * rotated * rotated
    correct_one = 1.0 - beta_one**step_count
    correct_two = 1.0 - beta_two**step_count
    scaled = split(first_val / correct_one / (jnp.sqrt(second_val / correct_two) + epsilon))
    for h in HALVES:
        back = dot3(scaled, (rt_hi[:, 128 * h : 128 * h + 128], rt_lo[:, 128 * h : 128 * h + 128]))
        change[h] = dot3((l_hi[...], l_lo[...]), split(back)).reshape(ND, 8, 128)
        coming[h][c, d] = change[h, d]
        for to in others:
            send(change.at[h, to], coming[h].at[c, d], e_sem.at[h], (to, s), 1)
    live = idx_ref[d, 0] > 0
    first_new[...] = jnp.where(live, first_val, first_old)
    second_new[...] = jnp.where(live, second_val, second_old)
    stores.append(pltpu.make_async_copy(first_new, first_out_hbm, out_sem.at[0]))
    stores.append(pltpu.make_async_copy(second_new, second_out_hbm, out_sem.at[1]))
    for store in stores:
        store.start()

    def share(h):
        arrived(coming[h].at[c, pl.ds(0, ND - 1)], e_sem.at[h])
        send(coming[h].at[c], coming[h].at[c], fs_sem.at[h], sibling, ND)

    def gather(kind, h):
        flat = coming[h].reshape(NC * ND, 8, 128)
        for zi in range(NZ):
            for blk in range(4):
                who = own_ref[0, (zi * NC + c) * 8 + 4 * kind + blk]
                tile = flat[(who & 1) * ND + (who >> 4)]
                mine[h, kind, zi, blk] = jnp.where(((who & (NS - 1)) >> 1) == z, tile, 0.0)

    def home_sends(kind, h):
        for k, via, i in ((-3, -1, 1), (3, 1, 0), (4, 2, 2), (1, 1, 3), (-1, -1, 4)):
            send(mine.at[h, kind, zs(k * f)], z_in.at[h, kind, i], f_sem.at[h, kind, i], at_z(via * f), 4)

    def home_relay(kind, h):
        for k, terms, i in ((-2, (1,), 6), (2, (0, 2), 5)):
            for j in terms:
                arrived(z_in.at[h, kind, j], f_sem.at[h, kind, j])
                mine[h, kind, zs(k * f)] += z_in[h, kind, j]
            send(mine.at[h, kind, zs(k * f)], z_in.at[h, kind, i], f_sem.at[h, kind, i], at_z(k * f), 4)

    def home_rows(kind, h):
        total = mine[h, kind, z]
        for i in (3, 4, 6, 5):
            arrived(z_in.at[h, kind, i], f_sem.at[h, kind, i])
            total += z_in[h, kind, i]
        old = params[4 * kind : 4 * kind + 4, :, 128 * h : 128 * h + 128]
        fresh[h, kind] = old - learn_rate * (total + decay_rate * old)

    def both_cores(h):
        yield at("b0", h)
        share(h)
        yield at("b00", h)
        arrived(coming[h].at[1 - c], fs_sem.at[h])

    def y_back(h):
        yield at("b1", h)
        gather(1, h)
        home_sends(1, h)
        yield at("b2", h)
        home_relay(1, h)
        yield at("b3", h)
        home_rows(1, h)
        pltpu.make_async_copy(fresh.at[h, 1], out_y(h, y, x), keep_sem.at[h, 1]).start()
        for k in (2, 1, 3):
            send(fresh.at[h, 1], out_y(h, y, x), gsx_sem.at[h], at_x(k), 4)
        yield at("b4", h)
        arrived(fresh.at[h, 1], keep_sem.at[h, 1])
        arrived(all_y(h, 0).at[:, pl.ds(0, NX - 1)], gsx_sem.at[h])
        send(all_y(h, y), all_y(h, y), gy_sem.at[h, 0], at_y(f), 16)
        send(all_y(h, y), all_y(h, y), gy_sem.at[h, 4], at_y(-f), 16)
        for step in range(4):
            yield at(f"g{step}", h)
            chunk = all_y(h, ys(-(step + 1) * f))
            arrived(chunk, gy_sem.at[h, step])
            if step < 3:
                send(chunk, chunk, gy_sem.at[h, step + 1], at_y(f), 16)
                chunk = all_y(h, ys((step + 1) * f))
                arrived(chunk, gy_sem.at[h, 4 + step])
                if step < 2:
                    send(chunk, chunk, gy_sem.at[h, 5 + step], at_y(-f), 16)

    def x_back(h):
        yield at("a0", h)
        gather(0, h)
        home_sends(0, h)
        yield at("a1", h)
        home_relay(0, h)
        yield at("a2", h)
        home_rows(0, h)
        pltpu.make_async_copy(fresh.at[h, 0], out_x(h, x, y), keep_sem.at[h, 0]).start()
        for k in (4, 3, 5, 2, 6, 1, 7):
            send(fresh.at[h, 0], out_x(h, x, y), gsy_sem.at[h], at_y(k), 4)
        yield at("a3", h)
        arrived(fresh.at[h, 0], keep_sem.at[h, 0])
        arrived(all_x(h, 0).at[:, pl.ds(0, NY - 1)], gsy_sem.at[h])
        send(all_x(h, x), all_x(h, x), gx_sem.at[h, 0], at_x(f), 32)
        send(all_x(h, x), all_x(h, x), gx_sem.at[h, 2], at_x(-f), 32)
        yield at("a4", h)
        chunk = all_x(h, xs(-f))
        arrived(chunk, gx_sem.at[h, 0])
        send(chunk, chunk, gx_sem.at[h, 1], at_x(f), 32)
        yield at("a5", h)
        arrived(all_x(h, xs(f)), gx_sem.at[h, 2])
        arrived(all_x(h, xs(2)), gx_sem.at[h, 1])

    in_order(both_cores(0), both_cores(1), y_back(0), y_back(1), x_back(0), x_back(1))
    finish()


def local(partials, params, left_basis, right_basis, first_moment, second_moment, owner_list):
    dma = pltpu.SemaphoreType.DMA
    full = (256, 256)
    vm = pltpu.VMEM
    any_spec = pl.BlockSpec(memory_space=pl.ANY)
    in_hbm = functools.partial(pltpu.with_memory_space_constraint, memory_space=pltpu.HBM)
    updated, first_out, second_out = pl.pallas_call(
        body,
        out_shape=(
            pltpu.VMEM((8, NY, NX, 8, 256), F32),
            pltpu.VMEM(full, F32),
            pltpu.VMEM(full, F32),
        ),
        in_specs=[any_spec] * 7,
        out_specs=(any_spec,) * 3,
        scratch_shapes=[
            vm((1, 128), jnp.int32), pltpu.SMEM((1, 128), jnp.int32), vm((ND, 128), jnp.int32), pltpu.SMEM((ND, 128), jnp.int32),
            vm((8, 256, 256), BF16), vm((8, 8, 256), F32),
            vm(full, F32), vm(full, F32), vm(full, F32), vm(full, F32), vm(full, F32), vm(full, F32),
            vm((2, NX, 4, NY, 8, 128), F32), vm((2, NY, 4, NX, 8, 128), F32),
            vm((2, 3, 4, NY, 8, 128), F32), vm((2, 7, 4, NX, 8, 128), F32),
            vm((2, NX - 1, 4, 8, 128), F32), vm((2, NY - 1, 4, 8, 128), F32),
            vm((2, NC, NZ, 4, 8, 128), F32), vm((2, NC, NZ, 4, 8, 128), F32),
            vm((2, ND, 8, 128), F32), vm((2, ND, 8, 128), F32),
            vm((2, ND, 8, 128), F32), vm((NC, ND, 8, 128), F32), vm((NC, ND, 8, 128), F32),
            vm((2, 2, NZ, 4, 8, 128), F32),
            vm((2, 2, NZ - 1, 4, 8, 128), F32), vm((2, 2, 4, 8, 128), F32),
            vm(full, BF16), vm(full, BF16), vm(full, BF16), vm(full, BF16),
            vm(full, BF16), vm(full, BF16), vm(full, BF16), vm(full, BF16),
            vm((3072, 8, 128), F32),
            dma((9,)), dma((1,)), dma((1,)), dma((2, 3)), dma((2, 7)), dma((2,)), dma((2,)), dma((2, 2, 7)), dma((2, 2)),
            dma((2,)), dma((2,)), dma((2,)), dma((2, 2, 7)), dma((2,)), dma((2,)), dma((2, 3)), dma((2, 7)), dma((2, 2)),
            dma((2,)),
        ],
        compiler_params=pltpu.CompilerParams(
            collective_id=0, has_side_effects=True, vmem_limit_bytes=48 * 1024 * 1024
        ),
        name="soap_step",
    )(
        *map(
            in_hbm,
            (
                owner_list.reshape(1, 128), partials[0], params, left_basis[0, 0, 0], right_basis[0, 0, 0],
                first_moment[0, 0, 0], second_moment[0, 0, 0],
            ),
        )
    )
    return (
        updated.reshape(8, 256, 256),
        first_out[None, None, None],
        second_out[None, None, None],
    )


def solution(mesh):
    return jax.shard_map(
        local,
        mesh=mesh,
        in_specs=(
            P("dp", "shard", None, None),
            P("shard", "dp", None),
            P("dp", "shard", None, None, None),
            P("dp", "shard", None, None, None),
            P("dp", "shard", None, None, None),
            P("dp", "shard", None, None, None),
            P(),
        ),
        out_specs=(
            P("shard", None, None),
            P("dp", "shard", None, None, None),
            P("dp", "shard", None, None, None),
        ),
        check_vma=False,
    )
```

```python
import functools

import jax
import jax.numpy as jnp
from jax import lax
from jax.experimental import pallas as pl
from jax.experimental.pallas import tpu as pltpu
from jax.sharding import PartitionSpec as P

beta_one = 0.9
beta_two = 0.95
epsilon = 1e-08
learn_rate = 0.2
decay_rate = 0.1
step_count = 10

MESH = pl.DeviceIdType.MESH
F32 = jnp.float32
BF16 = jnp.bfloat16
NX, NY, NZ, NC = 4, 8, 8, 2
ND, NS = NX * NY, NZ * NC
HALVES = (0, 1)

TIMES = {
    "x0": (5, 3),
    "x1": (9, 3),
    "x2": (14.8, 3.0),
    "x3": (18.1, 3.0),
    "x4": (21.6, 3.0),
    "y0": (3, 1.5),
    "y1": (6, 1.5),
    "y2": (9, 1.5),
    "y3": (12, 2),
    "y4": (15.0, 2.2),
    "y5": (18, 3.0),
    "y6": (21.5, 3.0),
    "c": (21.7, 3.0),
    "b0": (0, 2),
    "b00": (1.5, 2),
    "b1": (1.6, 2),
    "b2": (4.5, 2),
    "b3": (7.5, 2),
    "b4": (10.5, 2),
    "g0": (14.5, 1.5),
    "g1": (17.5, 1.5),
    "g2": (20.5, 1.5),
    "g3": (23.5, 1.5),
    "a0": (2.0, 2),
    "a1": (5.0, 2),
    "a2": (8.0, 2),
    "a25": (11.2, 2),
    "a3": (14.5, 2),
    "a4": (19, 2.5),
    "a5": (23, 2.5),
}


def at(step, half):
    start, later = TIMES[step]
    return start + later * half


def split(value):
    high = value.astype(BF16)
    return high, (value - high.astype(F32)).astype(BF16)


def dot(left, right):
    return jnp.dot(left, right, preferred_element_type=F32)


def dot3(left, right):
    return dot(left[0], right[0]) + (dot(left[0], right[1]) + dot(left[1], right[0]))


def body(
    own_hbm, part_hbm, params_hbm, left_hbm, right_hbm, first_hbm, second_hbm,
    out_hbm, first_out_hbm, second_out_hbm,
    own_vec, own_ref, idx_vec, idx_ref, part, params, left, right, first, second, first_new, second_new,
    acc_x, acc_y, in_x, in_y, small_x, small_y,
    every_0, every_1, chosen, whole, change, coming_0, coming_1, mine, z_in, fresh,
    l_hi, l_lo, lt_hi, lt_lo, r_hi, r_lo, rt_hi, rt_lo,
    meter, load_sem, idx_sem, send_sem, x_sem, y_sem, sx_sem, sy_sem, z_sem, zs_sem, c_sem, e_sem, fs_sem, f_sem,
    gsy_sem, gsx_sem, gx_sem, gy_sem, keep_sem, out_sem,
):
    d = lax.axis_index("dp")
    s = lax.axis_index("shard")
    y, x = lax.div(d, NX), lax.rem(d, NX)
    z, c = lax.div(s, NC), lax.rem(s, NC)
    f = 1 - 2 * c

    def xs(k):
        return lax.rem(x + k + 2 * NX, NX)

    def ys(k):
        return lax.rem(y + k + 2 * NY, NY)

    def zs(k):
        return lax.rem(z + k + NZ, NZ)

    def at_x(k):
        return (y * NX + xs(k), s)

    def at_y(k):
        return (ys(k) * NX + x, s)

    def at_z(k):
        return (d, zs(k) * NC + c)

    def at_d(k):
        return lax.rem(d + k, ND)

    others = [
        ys(j) * NX + xs(i)
        for j, i in sorted(
            ((j, i) for j in range(NY) for i in range(NX) if j or i),
            key=lambda to: -min(to[0], NY - to[0]) - min(to[1], NX - to[1]),
        )
    ]

    sibling = (d, z * NC + 1 - c)
    every = (every_0, every_1)
    coming = (coming_0, coming_1)
    sent = [0]
    stores = []

    def send(src, dst, recv, device, tiles):
        copy = pltpu.make_async_remote_copy(
            src_ref=src, dst_ref=dst, send_sem=send_sem.at[0], recv_sem=recv, device_id=device, device_id_type=MESH
        )
        copy.start()
        sent[0] += tiles

    def arrived(ref, sem):
        pltpu.make_async_copy(ref, ref, sem).wait()

    def block_at(slot_index):
        return jnp.maximum(idx_ref[slot_index, 0] - 1, 0)

    def finish():
        arrived(meter.at[pl.ds(0, sent[0])], send_sem.at[0])
        for store in stores:
            store.wait()

    def out_x(h, xi, yi):
        return out_hbm.at[pl.ds(0, 4), yi, xi, :, pl.ds(128 * h, 128)]

    def out_y(h, yi, xi):
        return out_hbm.at[pl.ds(4, 4), yi, xi, :, pl.ds(128 * h, 128)]

    def all_x(h, xi):
        return out_hbm.at[pl.ds(0, 4), :, xi, :, pl.ds(128 * h, 128)]

    def all_y(h, yi):
        return out_hbm.at[pl.ds(4, 4), yi, :, :, pl.ds(128 * h, 128)]

    def in_order(*streams):
        waiting = [(0.0, place, stream) for place, stream in enumerate(streams)]
        while waiting:
            waiting.sort(key=lambda entry: entry[:2])
            _, place, stream = waiting.pop(0)
            time = next(stream, None)
            if time is not None:
                waiting.append((time, place, stream))

    loads = [
        pltpu.make_async_copy(src, dst, load_sem.at[i])
        for i, (src, dst) in enumerate(
            (
                (own_hbm, own_vec), (part_hbm.at[pl.ds(4, 4)], part.at[pl.ds(4, 4)]),
                (part_hbm.at[pl.ds(0, 4)], part.at[pl.ds(0, 4)]),
                (left_hbm, left), (right_hbm, right), (first_hbm, first), (second_hbm, second), (params_hbm, params), (own_hbm, own_ref),
            )
        )
    ]
    for load in loads:
        load.start()

    barrier = pltpu.get_barrier_semaphore()
    for k in range(1, ND):
        pl.semaphore_signal(barrier, inc=1, device_id=(at_d(k), s), device_id_type=MESH)
    for k in range(1, NZ):
        pl.semaphore_signal(barrier, inc=1, device_id=at_z(k), device_id_type=MESH)
    pl.semaphore_signal(barrier, inc=1, device_id=sibling, device_id_type=MESH)

    loads[1].wait()

    @pl.loop(0, 4)
    def _(blk):
        for yi in range(NY):
            rows = part[4 + blk, 32 * yi : 32 * yi + 32, :].astype(F32)
            for xi in range(NX):
                for h in HALVES:
                    acc_y[h, yi, blk, xi] = rows[8 * xi : 8 * xi + 8, 128 * h : 128 * h + 128]

    pl.semaphore_wait(barrier, ND - 1 + NZ - 1 + 1)

    def spread(kind, h, total):
        own = every[h].at[kind, c, z]
        every[h][kind, c, z] = total
        for k, i in ((2, 0), (-2, 1), (1, 2), (-1, 3)):
            send(own, own, z_sem.at[h, kind, i], at_z(k * f), 4)
        send(own, own, zs_sem.at[h, kind], sibling, 4)

    def relay(kind, h):
        for k, i, onward in ((-2, 0, ((2, 6), (1, 4))), (2, 1, ((-1, 5),)), (-1, 2, ()), (1, 3, ())):
            chunk = every[h].at[kind, c, zs(k * f)]
            arrived(chunk, z_sem.at[h, kind, i])
            for via, j in onward:
                send(chunk, chunk, z_sem.at[h, kind, j], at_z(via * f), 4)
            send(chunk, chunk, zs_sem.at[h, kind], sibling, 4)

    def relay_far(kind, h):
        for k, i in ((-3, 4), (3, 5), (4, 6)):
            chunk = every[h].at[kind, c, zs(k * f)]
            arrived(chunk, z_sem.at[h, kind, i])
            send(chunk, chunk, zs_sem.at[h, kind], sibling, 4)

    def x_blocks():
        loads[2].wait()

        @pl.loop(0, 4)
        def _(blk):
            for yi in range(NY):
                rows = part[blk, 32 * yi : 32 * yi + 32, :].astype(F32)
                for xi in range(NX):
                    for h in HALVES:
                        acc_x[h, xi, blk, yi] = rows[8 * xi : 8 * xi + 8, 128 * h : 128 * h + 128]
        yield from ()

    def x_unit(h):
        send(acc_x.at[h, xs(2)], in_x.at[h, 0], x_sem.at[h, 0], at_x(f), 32)
        send(acc_x.at[h, xs(-f)], in_x.at[h, 2], x_sem.at[h, 2], at_x(-f), 32)
        yield at("x0", h)
        arrived(in_x.at[h, 0], x_sem.at[h, 0])
        acc_x[h, xs(f)] += in_x[h, 0]
        send(acc_x.at[h, xs(f)], in_x.at[h, 1], x_sem.at[h, 1], at_x(f), 32)
        yield at("x1", h)
        arrived(in_x.at[h, 2], x_sem.at[h, 2])
        arrived(in_x.at[h, 1], x_sem.at[h, 1])
        acc_x[h, x] += in_x[h, 1] + in_x[h, 2]
        for k in (4, 3, 5, 2, 6, 1, 7):
            send(acc_x.at[h, x, :, ys(k)], small_y.at[h, k - 1], sy_sem.at[h], at_y(k), 4)
        yield at("x2", h)
        arrived(small_y.at[h], sy_sem.at[h])
        total = acc_x[h, x, :, y]
        for k in range(NY - 1):
            total += small_y[h, k]
        spread(0, h, total)
        yield at("x3", h)
        relay(0, h)
        yield at("x4", h)
        relay_far(0, h)

    def y_unit(h):
        send(acc_y.at[h, ys(4)], in_y.at[h, 0], y_sem.at[h, 0], at_y(f), 16)
        send(acc_y.at[h, ys(-3 * f)], in_y.at[h, 4], y_sem.at[h, 4], at_y(-f), 16)
        for step in range(3):
            yield at(f"y{step}", h)
            arrived(in_y.at[h, step], y_sem.at[h, step])
            far = ys((3 - step) * f)
            acc_y[h, far] += in_y[h, step]
            send(acc_y.at[h, far], in_y.at[h, step + 1], y_sem.at[h, step + 1], at_y(f), 16)
            if step < 2:
                arrived(in_y.at[h, 4 + step], y_sem.at[h, 4 + step])
                far = ys(-(2 - step) * f)
                acc_y[h, far] += in_y[h, 4 + step]
                send(acc_y.at[h, far], in_y.at[h, 5 + step], y_sem.at[h, 5 + step], at_y(-f), 16)
        yield at("y3", h)
        arrived(in_y.at[h, 3], y_sem.at[h, 3])
        arrived(in_y.at[h, 6], y_sem.at[h, 6])
        acc_y[h, y] += in_y[h, 3] + in_y[h, 6]
        for k in (2, 1, 3):
            send(acc_y.at[h, y, :, xs(k)], small_x.at[h, k - 1], sx_sem.at[h], at_x(k), 4)
        yield at("y4", h)
        arrived(small_x.at[h], sx_sem.at[h])
        total = acc_y[h, y, :, x]
        for k in range(NX - 1):
            total += small_x[h, k]
        spread(1, h, total)
        yield at("y5", h)
        relay(1, h)
        yield at("y6", h)
        relay_far(1, h)

    def bases():
        yield 2.0
        loads[0].wait()
        block = lax.broadcasted_iota(jnp.int32, (ND, 128), 1)
        home, inner = lax.div(block, 8), lax.rem(block, 8)
        place = ((lax.div(inner, 4) * NC + lax.rem(home, NC)) * NZ + lax.div(home, NC)) * 4 + lax.rem(inner, 4) + 1
        slot = lax.broadcasted_iota(jnp.int32, (ND, 128), 0) * NS + s
        found = jnp.max(jnp.where(own_vec[...] == slot, place, 0), axis=1, keepdims=True)
        idx_vec[...] = jnp.broadcast_to(found, (ND, 128))
        idx_copy = pltpu.make_async_copy(idx_vec, idx_ref, idx_sem.at[0])
        idx_copy.start()
        for load in loads[3:]:
            load.wait()
        value = left[...]
        l_hi[...], l_lo[...] = split(value)
        yield 2.1
        lt_hi[...], lt_lo[...] = split(left[...].T)
        yield 5.0
        value = right[...]
        r_hi[...], r_lo[...] = split(value)
        yield 8.0
        rt_hi[...], rt_lo[...] = split(right[...].T)
        idx_copy.wait()

    def to_owners(h):
        yield at("c", h)
        for kind in range(2):
            arrived(every[h].at[kind, 1 - c], zs_sem.at[h, kind])
        flat = every[h].reshape(128, 8, 128)
        whole[h, d] = flat[block_at(d)]
        for to in others:
            chosen[h, to] = flat[block_at(to)]
            send(chosen.at[h, to], whole.at[h, d], c_sem.at[h], (to, s), 1)

    in_order(y_unit(0), y_unit(1), x_blocks(), x_unit(0), x_unit(1), bases(), to_owners(0), to_owners(1))

    rotated = 0.0
    for h in HALVES:
        arrived(whole.at[h, pl.ds(0, ND - 1)], c_sem.at[h])
        partway = dot3((lt_hi[...], lt_lo[...]), split(whole[h].reshape(256, 128)))
        rows = slice(128 * h, 128 * h + 128)
        rotated += dot3(split(partway), (r_hi[rows], r_lo[rows]))
    first_old, second_old = first[...], second[...]
    first_val = beta_one * first_old + (1.0 - beta_one) * rotated
    second_val = beta_two * second_old + (1.0 - beta_two) * rotated * rotated
    correct_one = 1.0 - beta_one**step_count
    correct_two = 1.0 - beta_two**step_count
    scaled = split(first_val / correct_one / (jnp.sqrt(second_val / correct_two) + epsilon))
    for h in HALVES:
        back = dot3(scaled, (rt_hi[:, 128 * h : 128 * h + 128], rt_lo[:, 128 * h : 128 * h + 128]))
        change[h] = dot3((l_hi[...], l_lo[...]), split(back)).reshape(ND, 8, 128)
        coming[h][c, d] = change[h, d]
        for to in others:
            send(change.at[h, to], coming[h].at[c, d], e_sem.at[h], (to, s), 1)
    live = idx_ref[d, 0] > 0
    first_new[...] = jnp.where(live, first_val, first_old)
    second_new[...] = jnp.where(live, second_val, second_old)
    stores.append(pltpu.make_async_copy(first_new, first_out_hbm, out_sem.at[0]))
    stores.append(pltpu.make_async_copy(second_new, second_out_hbm, out_sem.at[1]))
    for store in stores:
        store.start()

    def share(h):
        arrived(coming[h].at[c, pl.ds(0, ND - 1)], e_sem.at[h])
        send(coming[h].at[c], coming[h].at[c], fs_sem.at[h], sibling, ND)

    def gather(kind, h):
        flat = coming[h].reshape(NC * ND, 8, 128)
        for zi in range(NZ):
            for blk in range(4):
                who = own_ref[0, (zi * NC + c) * 8 + 4 * kind + blk]
                tile = flat[(who & 1) * ND + (who >> 4)]
                mine[h, kind, zi, blk] = jnp.where(((who & (NS - 1)) >> 1) == z, tile, 0.0)

    def home_sends(kind, h):
        for k, via, i in ((-3, -1, 1), (3, 1, 0), (4, 2, 2), (1, 1, 3), (-1, -1, 4)):
            send(mine.at[h, kind, zs(k * f)], z_in.at[h, kind, i], f_sem.at[h, kind, i], at_z(via * f), 4)

    def home_relay(kind, h):
        for k, terms, i in ((-2, (1,), 6), (2, (0, 2), 5)):
            for j in terms:
                arrived(z_in.at[h, kind, j], f_sem.at[h, kind, j])
                mine[h, kind, zs(k * f)] += z_in[h, kind, j]
            send(mine.at[h, kind, zs(k * f)], z_in.at[h, kind, i], f_sem.at[h, kind, i], at_z(k * f), 4)

    def home_rows(kind, h):
        total = mine[h, kind, z]
        for i in (3, 4, 6, 5):
            arrived(z_in.at[h, kind, i], f_sem.at[h, kind, i])
            total += z_in[h, kind, i]
        old = params[4 * kind : 4 * kind + 4, :, 128 * h : 128 * h + 128]
        fresh[h, kind] = old - learn_rate * (total + decay_rate * old)

    def both_cores(h):
        yield at("b0", h)
        share(h)
        yield at("b00", h)
        arrived(coming[h].at[1 - c], fs_sem.at[h])

    def y_back(h):
        yield at("b1", h)
        gather(1, h)
        home_sends(1, h)
        yield at("b2", h)
        home_relay(1, h)
        yield at("b3", h)
        home_rows(1, h)
        pltpu.make_async_copy(fresh.at[h, 1], out_y(h, y, x), keep_sem.at[h, 1]).start()
        for k in (2, 1, 3):
            send(fresh.at[h, 1], out_y(h, y, x), gsx_sem.at[h], at_x(k), 4)
        yield at("b4", h)
        arrived(fresh.at[h, 1], keep_sem.at[h, 1])
        arrived(all_y(h, 0).at[:, pl.ds(0, NX - 1)], gsx_sem.at[h])
        send(all_y(h, y), all_y(h, y), gy_sem.at[h, 0], at_y(f), 16)
        send(all_y(h, y), all_y(h, y), gy_sem.at[h, 4], at_y(-f), 16)
        for step in range(4):
            yield at(f"g{step}", h)
            chunk = all_y(h, ys(-(step + 1) * f))
            arrived(chunk, gy_sem.at[h, step])
            if step < 3:
                send(chunk, chunk, gy_sem.at[h, step + 1], at_y(f), 16)
                chunk = all_y(h, ys((step + 1) * f))
                arrived(chunk, gy_sem.at[h, 4 + step])
                if step < 2:
                    send(chunk, chunk, gy_sem.at[h, 5 + step], at_y(-f), 16)

    def x_back(h):
        yield at("a0", h)
        gather(0, h)
        home_sends(0, h)
        yield at("a1", h)
        home_relay(0, h)
        yield at("a2", h)
        home_rows(0, h)
        pltpu.make_async_copy(fresh.at[h, 0], out_x(h, x, y), keep_sem.at[h, 0]).start()
        for k, i in ((2, 0), (-2, 1), (1, 2), (-1, 3)):
            send(fresh.at[h, 0], out_x(h, x, y), gsy_sem.at[h, i], at_y(k * f), 4)
        yield at("a25", h)
        for k, i, onward in ((-2, 0, ((2, 6), (1, 4))), (2, 1, ((-1, 5),))):
            chunk = out_x(h, x, ys(k * f))
            arrived(chunk, gsy_sem.at[h, i])
            for via, j in onward:
                send(chunk, chunk, gsy_sem.at[h, j], at_y(via * f), 4)
        yield at("a3", h)
        arrived(fresh.at[h, 0], keep_sem.at[h, 0])
        for k, i in ((-1, 2), (1, 3), (-3, 4), (3, 5), (4, 6)):
            arrived(out_x(h, x, ys(k * f)), gsy_sem.at[h, i])
        send(all_x(h, x), all_x(h, x), gx_sem.at[h, 0], at_x(f), 32)
        send(all_x(h, x), all_x(h, x), gx_sem.at[h, 2], at_x(-f), 32)
        yield at("a4", h)
        chunk = all_x(h, xs(-f))
        arrived(chunk, gx_sem.at[h, 0])
        send(chunk, chunk, gx_sem.at[h, 1], at_x(f), 32)
        yield at("a5", h)
        arrived(all_x(h, xs(f)), gx_sem.at[h, 2])
        arrived(all_x(h, xs(2)), gx_sem.at[h, 1])

    in_order(both_cores(0), both_cores(1), y_back(0), y_back(1), x_back(0), x_back(1))
    finish()


def local(partials, params, left_basis, right_basis, first_moment, second_moment, owner_list):
    dma = pltpu.SemaphoreType.DMA
    full = (256, 256)
    vm = pltpu.VMEM
    any_spec = pl.BlockSpec(memory_space=pl.ANY)
    in_hbm = functools.partial(pltpu.with_memory_space_constraint, memory_space=pltpu.HBM)
    updated, first_out, second_out = pl.pallas_call(
        body,
        out_shape=(
            pltpu.VMEM((8, NY, NX, 8, 256), F32),
            pltpu.VMEM(full, F32),
            pltpu.VMEM(full, F32),
        ),
        in_specs=[any_spec] * 7,
        out_specs=(any_spec,) * 3,
        scratch_shapes=[
            vm((1, 128), jnp.int32), pltpu.SMEM((1, 128), jnp.int32), vm((ND, 128), jnp.int32), pltpu.SMEM((ND, 128), jnp.int32),
            vm((8, 256, 256), BF16), vm((8, 8, 256), F32),
            vm(full, F32), vm(full, F32), vm(full, F32), vm(full, F32), vm(full, F32), vm(full, F32),
            vm((2, NX, 4, NY, 8, 128), F32), vm((2, NY, 4, NX, 8, 128), F32),
            vm((2, 3, 4, NY, 8, 128), F32), vm((2, 7, 4, NX, 8, 128), F32),
            vm((2, NX - 1, 4, 8, 128), F32), vm((2, NY - 1, 4, 8, 128), F32),
            vm((2, NC, NZ, 4, 8, 128), F32), vm((2, NC, NZ, 4, 8, 128), F32),
            vm((2, ND, 8, 128), F32), vm((2, ND, 8, 128), F32),
            vm((2, ND, 8, 128), F32), vm((NC, ND, 8, 128), F32), vm((NC, ND, 8, 128), F32),
            vm((2, 2, NZ, 4, 8, 128), F32),
            vm((2, 2, NZ - 1, 4, 8, 128), F32), vm((2, 2, 4, 8, 128), F32),
            vm(full, BF16), vm(full, BF16), vm(full, BF16), vm(full, BF16),
            vm(full, BF16), vm(full, BF16), vm(full, BF16), vm(full, BF16),
            vm((3072, 8, 128), F32),
            dma((9,)), dma((1,)), dma((1,)), dma((2, 3)), dma((2, 7)), dma((2,)), dma((2,)), dma((2, 2, 7)), dma((2, 2)),
            dma((2,)), dma((2,)), dma((2,)), dma((2, 2, 7)), dma((2, 7)), dma((2,)), dma((2, 3)), dma((2, 7)), dma((2, 2)),
            dma((2,)),
        ],
        compiler_params=pltpu.CompilerParams(
            collective_id=0, has_side_effects=True, vmem_limit_bytes=48 * 1024 * 1024
        ),
        name="soap_step",
    )(
        *map(
            in_hbm,
            (
                owner_list.reshape(1, 128), partials[0], params, left_basis[0, 0, 0], right_basis[0, 0, 0],
                first_moment[0, 0, 0], second_moment[0, 0, 0],
            ),
        )
    )
    return (
        updated.reshape(8, 256, 256),
        first_out[None, None, None],
        second_out[None, None, None],
    )


def solution(mesh):
    return jax.shard_map(
        local,
        mesh=mesh,
        in_specs=(
            P("dp", "shard", None, None),
            P("shard", "dp", None),
            P("dp", "shard", None, None, None),
            P("dp", "shard", None, None, None),
            P("dp", "shard", None, None, None),
            P("dp", "shard", None, None, None),
            P(),
        ),
        out_specs=(
            P("shard", None, None),
            P("dp", "shard", None, None, None),
            P("dp", "shard", None, None, None),
        ),
        check_vma=False,
    )
```

```python
import functools

import jax
import jax.numpy as jnp
from jax import lax
from jax.experimental import pallas as pl
from jax.experimental.pallas import tpu as pltpu
from jax.sharding import PartitionSpec as P

beta_one = 0.9
beta_two = 0.95
epsilon = 1e-08
learn_rate = 0.2
decay_rate = 0.1
step_count = 10

MESH = pl.DeviceIdType.MESH
F32 = jnp.float32
BF16 = jnp.bfloat16
NX, NY, NZ, NC = 4, 8, 8, 2
ND, NS = NX * NY, NZ * NC
HALVES = (0, 1)

TIMES = {
    "x0": (5, 3),
    "x1": (9, 3),
    "x2": (14.8, 3.0),
    "x3": (18.1, 3.0),
    "x4": (21.6, 3.0),
    "y0": (3, 1.5),
    "y1": (6, 1.5),
    "y2": (9, 1.5),
    "y3": (12, 2),
    "y4": (15.0, 2.2),
    "y5": (18, 3.0),
    "y6": (21.5, 3.0),
    "c": (21.7, 3.0),
    "b0": (0, 2),
    "b00": (1.5, 2),
    "b1": (1.6, 2),
    "b2": (4.5, 2),
    "b3": (7.5, 2),
    "b4": (10.5, 2),
    "g0": (14.5, 1.5),
    "g1": (17.5, 1.5),
    "g2": (20.5, 1.5),
    "g3": (23.5, 1.5),
    "a0": (2.0, 2),
    "a1": (5.0, 2),
    "a2": (8.0, 2),
    "a25": (11.2, 2),
    "a3": (14.5, 2),
    "a4": (19, 2.5),
    "a5": (23, 2.5),
}


def at(step, half):
    start, later = TIMES[step]
    return start + later * half


def split(value):
    high = value.astype(BF16)
    return high, (value - high.astype(F32)).astype(BF16)


def dot(left, right):
    return jnp.dot(left, right, preferred_element_type=F32)


def dot3(left, right):
    return dot(left[0], right[0]) + (dot(left[0], right[1]) + dot(left[1], right[0]))


def body(
    own_hbm, part_hbm, params_hbm, left_hbm, right_hbm, first_hbm, second_hbm,
    out_hbm, first_out_hbm, second_out_hbm,
    own_vec, own_ref, idx_vec, idx_ref, part, params, left, right, first, second, first_new, second_new,
    acc_x, acc_y, in_x, in_y, small_x, small_y,
    every_0, every_1, chosen, whole, change, coming_0, coming_1, mine, z_in, fresh,
    l_hi, l_lo, lt_hi, lt_lo, r_hi, r_lo, rt_hi, rt_lo,
    meter, load_sem, idx_sem, send_sem, x_sem, y_sem, sx_sem, sy_sem, z_sem, zs_sem, c_sem, e_sem, fs_sem, f_sem,
    gsy_sem, gsx_sem, gx_sem, gy_sem, keep_sem, out_sem,
):
    d = lax.axis_index("dp")
    s = lax.axis_index("shard")
    y, x = lax.div(d, NX), lax.rem(d, NX)
    z, c = lax.div(s, NC), lax.rem(s, NC)
    f = 1 - 2 * c

    def xs(k):
        return lax.rem(x + k + 2 * NX, NX)

    def ys(k):
        return lax.rem(y + k + 2 * NY, NY)

    def zs(k):
        return lax.rem(z + k + NZ, NZ)

    def at_x(k):
        return (y * NX + xs(k), s)

    def at_y(k):
        return (ys(k) * NX + x, s)

    def at_z(k):
        return (d, zs(k) * NC + c)

    def at_d(k):
        return lax.rem(d + k, ND)

    others = [
        ys(j) * NX + xs(i)
        for j, i in sorted(
            ((j, i) for j in range(NY) for i in range(NX) if j or i),
            key=lambda to: -min(to[0], NY - to[0]) - min(to[1], NX - to[1]),
        )
    ]

    sibling = (d, z * NC + 1 - c)
    every = (every_0, every_1)
    coming = (coming_0, coming_1)
    sent = [0]
    stores = []

    def send(src, dst, recv, device, tiles):
        copy = pltpu.make_async_remote_copy(
            src_ref=src, dst_ref=dst, send_sem=send_sem.at[0], recv_sem=recv, device_id=device, device_id_type=MESH
        )
        copy.start()
        sent[0] += tiles

    def arrived(ref, sem):
        pltpu.make_async_copy(ref, ref, sem).wait()

    def block_at(slot_index):
        return jnp.maximum(idx_ref[slot_index, 0] - 1, 0)

    def finish():
        arrived(meter.at[pl.ds(0, sent[0])], send_sem.at[0])
        for store in stores:
            store.wait()

    def out_x(h, xi, yi):
        return out_hbm.at[pl.ds(0, 4), yi, xi, :, pl.ds(128 * h, 128)]

    def out_y(h, yi, xi):
        return out_hbm.at[pl.ds(4, 4), yi, xi, :, pl.ds(128 * h, 128)]

    def all_x(h, xi):
        return out_hbm.at[pl.ds(0, 4), :, xi, :, pl.ds(128 * h, 128)]

    def all_y(h, yi):
        return out_hbm.at[pl.ds(4, 4), yi, :, :, pl.ds(128 * h, 128)]

    def in_order(*streams):
        waiting = [(0.0, place, stream) for place, stream in enumerate(streams)]
        while waiting:
            waiting.sort(key=lambda entry: entry[:2])
            _, place, stream = waiting.pop(0)
            time = next(stream, None)
            if time is not None:
                waiting.append((time, place, stream))

    loads = [
        pltpu.make_async_copy(src, dst, load_sem.at[i])
        for i, (src, dst) in enumerate(
            (
                (own_hbm, own_vec), (part_hbm.at[pl.ds(4, 4)], part.at[pl.ds(4, 4)]),
                (part_hbm.at[pl.ds(0, 4)], part.at[pl.ds(0, 4)]),
                (left_hbm, left), (right_hbm, right), (first_hbm, first), (second_hbm, second), (params_hbm, params), (own_hbm, own_ref),
            )
        )
    ]
    for load in loads:
        load.start()

    barrier = pltpu.get_barrier_semaphore()
    for k in range(1, ND):
        pl.semaphore_signal(barrier, inc=1, device_id=(at_d(k), s), device_id_type=MESH)
    for k in range(1, NZ):
        pl.semaphore_signal(barrier, inc=1, device_id=at_z(k), device_id_type=MESH)
    pl.semaphore_signal(barrier, inc=1, device_id=sibling, device_id_type=MESH)

    loads[1].wait()

    @pl.loop(0, 4)
    def _(blk):
        for yi in range(NY):
            rows = part[4 + blk, 32 * yi : 32 * yi + 32, :].astype(F32)
            for xi in range(NX):
                for h in HALVES:
                    acc_y[h, yi, blk, xi] = rows[8 * xi : 8 * xi + 8, 128 * h : 128 * h + 128]

    pl.semaphore_wait(barrier, ND - 1 + NZ - 1 + 1)

    def spread(kind, h, total):
        own = every[h].at[kind, c, z]
        every[h][kind, c, z] = total
        for k, i in ((2, 0), (-2, 1), (1, 2), (-1, 3)):
            send(own, own, z_sem.at[h, kind, i], at_z(k * f), 4)
        send(own, own, zs_sem.at[h, kind], sibling, 4)

    def relay(kind, h):
        for k, i, onward in ((-2, 0, ((2, 6), (1, 4))), (2, 1, ((-1, 5),)), (-1, 2, ()), (1, 3, ())):
            chunk = every[h].at[kind, c, zs(k * f)]
            arrived(chunk, z_sem.at[h, kind, i])
            for via, j in onward:
                send(chunk, chunk, z_sem.at[h, kind, j], at_z(via * f), 4)
            send(chunk, chunk, zs_sem.at[h, kind], sibling, 4)

    def relay_far(kind, h):
        for k, i in ((-3, 4), (3, 5), (4, 6)):
            chunk = every[h].at[kind, c, zs(k * f)]
            arrived(chunk, z_sem.at[h, kind, i])
            send(chunk, chunk, zs_sem.at[h, kind], sibling, 4)

    def x_blocks():
        loads[2].wait()

        @pl.loop(0, 4)
        def _(blk):
            for yi in range(NY):
                rows = part[blk, 32 * yi : 32 * yi + 32, :].astype(F32)
                for xi in range(NX):
                    for h in HALVES:
                        acc_x[h, xi, blk, yi] = rows[8 * xi : 8 * xi + 8, 128 * h : 128 * h + 128]
        yield from ()

    def x_unit(h):
        send(acc_x.at[h, xs(2)], in_x.at[h, 0], x_sem.at[h, 0], at_x(f), 32)
        send(acc_x.at[h, xs(-f)], in_x.at[h, 2], x_sem.at[h, 2], at_x(-f), 32)
        yield at("x0", h)
        arrived(in_x.at[h, 0], x_sem.at[h, 0])
        acc_x[h, xs(f)] += in_x[h, 0]
        send(acc_x.at[h, xs(f)], in_x.at[h, 1], x_sem.at[h, 1], at_x(f), 32)
        yield at("x1", h)
        arrived(in_x.at[h, 2], x_sem.at[h, 2])
        arrived(in_x.at[h, 1], x_sem.at[h, 1])
        acc_x[h, x] += in_x[h, 1] + in_x[h, 2]
        for k in (4, 3, 5, 2, 6, 1, 7):
            send(acc_x.at[h, x, :, ys(k)], small_y.at[h, k - 1], sy_sem.at[h], at_y(k), 4)
        yield at("x2", h)
        arrived(small_y.at[h], sy_sem.at[h])
        total = acc_x[h, x, :, y]
        for k in range(NY - 1):
            total += small_y[h, k]
        spread(0, h, total)
        yield at("x3", h)
        relay(0, h)
        yield at("x4", h)
        relay_far(0, h)

    def y_unit(h):
        send(acc_y.at[h, ys(4)], in_y.at[h, 0], y_sem.at[h, 0], at_y(f), 16)
        send(acc_y.at[h, ys(-3 * f)], in_y.at[h, 4], y_sem.at[h, 4], at_y(-f), 16)
        for step in range(3):
            yield at(f"y{step}", h)
            arrived(in_y.at[h, step], y_sem.at[h, step])
            far = ys((3 - step) * f)
            acc_y[h, far] += in_y[h, step]
            send(acc_y.at[h, far], in_y.at[h, step + 1], y_sem.at[h, step + 1], at_y(f), 16)
            if step < 2:
                arrived(in_y.at[h, 4 + step], y_sem.at[h, 4 + step])
                far = ys(-(2 - step) * f)
                acc_y[h, far] += in_y[h, 4 + step]
                send(acc_y.at[h, far], in_y.at[h, 5 + step], y_sem.at[h, 5 + step], at_y(-f), 16)
        yield at("y3", h)
        arrived(in_y.at[h, 3], y_sem.at[h, 3])
        arrived(in_y.at[h, 6], y_sem.at[h, 6])
        acc_y[h, y] += in_y[h, 3] + in_y[h, 6]
        for k in (2, 1, 3):
            send(acc_y.at[h, y, :, xs(k)], small_x.at[h, k - 1], sx_sem.at[h], at_x(k), 4)
        yield at("y4", h)
        arrived(small_x.at[h], sx_sem.at[h])
        total = acc_y[h, y, :, x]
        for k in range(NX - 1):
            total += small_x[h, k]
        spread(1, h, total)
        yield at("y5", h)
        relay(1, h)
        yield at("y6", h)
        relay_far(1, h)

    def bases():
        yield 2.0
        loads[0].wait()
        block = lax.broadcasted_iota(jnp.int32, (ND, 128), 1)
        home, inner = lax.div(block, 8), lax.rem(block, 8)
        place = ((lax.div(inner, 4) * NC + lax.rem(home, NC)) * NZ + lax.div(home, NC)) * 4 + lax.rem(inner, 4) + 1
        slot = lax.broadcasted_iota(jnp.int32, (ND, 128), 0) * NS + s
        found = jnp.max(jnp.where(own_vec[...] == slot, place, 0), axis=1, keepdims=True)
        idx_vec[...] = jnp.broadcast_to(found, (ND, 128))
        idx_copy = pltpu.make_async_copy(idx_vec, idx_ref, idx_sem.at[0])
        idx_copy.start()
        for load in loads[3:]:
            load.wait()
        value = left[...]
        l_hi[...], l_lo[...] = split(value)
        yield 2.1
        lt_hi[...], lt_lo[...] = split(left[...].T)
        yield 5.0
        value = right[...]
        r_hi[...], r_lo[...] = split(value)
        yield 8.0
        rt_hi[...], rt_lo[...] = split(right[...].T)
        idx_copy.wait()

    def to_owners(h):
        yield at("c", h)
        for kind in range(2):
            arrived(every[h].at[kind, 1 - c], zs_sem.at[h, kind])
        flat = every[h].reshape(128, 8, 128)
        whole[h, d] = flat[block_at(d)]
        for to in others:
            chosen[h, to] = flat[block_at(to)]
            send(chosen.at[h, to], whole.at[h, d], c_sem.at[h], (to, s), 1)

    in_order(y_unit(0), y_unit(1), x_blocks(), x_unit(0), x_unit(1), bases(), to_owners(0), to_owners(1))

    rotated = 0.0
    for h in HALVES:
        arrived(whole.at[h, pl.ds(0, ND - 1)], c_sem.at[h])
        partway = dot3((lt_hi[...], lt_lo[...]), split(whole[h].reshape(256, 128)))
        rows = slice(128 * h, 128 * h + 128)
        rotated += dot3(split(partway), (r_hi[rows], r_lo[rows]))
    first_old, second_old = first[...], second[...]
    first_val = beta_one * first_old + (1.0 - beta_one) * rotated
    second_val = beta_two * second_old + (1.0 - beta_two) * rotated * rotated
    correct_one = 1.0 - beta_one**step_count
    correct_two = 1.0 - beta_two**step_count
    scaled = split(first_val * (1.0 / correct_one) / (jnp.sqrt(second_val * (1.0 / correct_two)) + epsilon))
    for h in HALVES:
        back = dot3(scaled, (rt_hi[:, 128 * h : 128 * h + 128], rt_lo[:, 128 * h : 128 * h + 128]))
        change[h] = dot3((l_hi[...], l_lo[...]), split(back)).reshape(ND, 8, 128)
        coming[h][c, d] = change[h, d]
        for to in others:
            send(change.at[h, to], coming[h].at[c, d], e_sem.at[h], (to, s), 1)
    live = idx_ref[d, 0] > 0
    first_new[...] = jnp.where(live, first_val, first_old)
    second_new[...] = jnp.where(live, second_val, second_old)
    stores.append(pltpu.make_async_copy(first_new, first_out_hbm, out_sem.at[0]))
    stores.append(pltpu.make_async_copy(second_new, second_out_hbm, out_sem.at[1]))
    for store in stores:
        store.start()

    def share(h):
        arrived(coming[h].at[c, pl.ds(0, ND - 1)], e_sem.at[h])
        send(coming[h].at[c], coming[h].at[c], fs_sem.at[h], sibling, ND)

    def gather(kind, h):
        flat = coming[h].reshape(NC * ND, 8, 128)
        @pl.loop(0, NZ)
        def _(zi):
            for blk in range(4):
                who = own_ref[0, (zi * NC + c) * 8 + 4 * kind + blk]
                tile = flat[(who & 1) * ND + (who >> 4)]
                mine[h, kind, zi, blk] = jnp.where(((who & (NS - 1)) >> 1) == z, tile, 0.0)

    def home_sends(kind, h):
        for k, via, i in ((-3, -1, 1), (3, 1, 0), (4, 2, 2), (1, 1, 3), (-1, -1, 4)):
            send(mine.at[h, kind, zs(k * f)], z_in.at[h, kind, i], f_sem.at[h, kind, i], at_z(via * f), 4)

    def home_relay(kind, h):
        for k, terms, i in ((-2, (1,), 6), (2, (0, 2), 5)):
            for j in terms:
                arrived(z_in.at[h, kind, j], f_sem.at[h, kind, j])
                mine[h, kind, zs(k * f)] += z_in[h, kind, j]
            send(mine.at[h, kind, zs(k * f)], z_in.at[h, kind, i], f_sem.at[h, kind, i], at_z(k * f), 4)

    def home_rows(kind, h):
        total = mine[h, kind, z]
        for i in (3, 4, 6, 5):
            arrived(z_in.at[h, kind, i], f_sem.at[h, kind, i])
            total += z_in[h, kind, i]
        old = params[4 * kind : 4 * kind + 4, :, 128 * h : 128 * h + 128]
        fresh[h, kind] = old - learn_rate * (total + decay_rate * old)

    def both_cores(h):
        yield at("b0", h)
        share(h)
        yield at("b00", h)
        arrived(coming[h].at[1 - c], fs_sem.at[h])

    def y_back(h):
        yield at("b1", h)
        gather(1, h)
        home_sends(1, h)
        yield at("b2", h)
        home_relay(1, h)
        yield at("b3", h)
        home_rows(1, h)
        pltpu.make_async_copy(fresh.at[h, 1], out_y(h, y, x), keep_sem.at[h, 1]).start()
        for k in (2, 1, 3):
            send(fresh.at[h, 1], out_y(h, y, x), gsx_sem.at[h], at_x(k), 4)
        yield at("b4", h)
        arrived(fresh.at[h, 1], keep_sem.at[h, 1])
        arrived(all_y(h, 0).at[:, pl.ds(0, NX - 1)], gsx_sem.at[h])
        send(all_y(h, y), all_y(h, y), gy_sem.at[h, 0], at_y(f), 16)
        send(all_y(h, y), all_y(h, y), gy_sem.at[h, 4], at_y(-f), 16)
        for step in range(4):
            yield at(f"g{step}", h)
            chunk = all_y(h, ys(-(step + 1) * f))
            arrived(chunk, gy_sem.at[h, step])
            if step < 3:
                send(chunk, chunk, gy_sem.at[h, step + 1], at_y(f), 16)
                chunk = all_y(h, ys((step + 1) * f))
                arrived(chunk, gy_sem.at[h, 4 + step])
                if step < 2:
                    send(chunk, chunk, gy_sem.at[h, 5 + step], at_y(-f), 16)

    def x_back(h):
        yield at("a0", h)
        gather(0, h)
        home_sends(0, h)
        yield at("a1", h)
        home_relay(0, h)
        yield at("a2", h)
        home_rows(0, h)
        pltpu.make_async_copy(fresh.at[h, 0], out_x(h, x, y), keep_sem.at[h, 0]).start()
        for k, i in ((2, 0), (-2, 1), (1, 2), (-1, 3)):
            send(fresh.at[h, 0], out_x(h, x, y), gsy_sem.at[h, i], at_y(k * f), 4)
        yield at("a25", h)
        for k, i, onward in ((-2, 0, ((2, 6), (1, 4))), (2, 1, ((-1, 5),))):
            chunk = out_x(h, x, ys(k * f))
            arrived(chunk, gsy_sem.at[h, i])
            for via, j in onward:
                send(chunk, chunk, gsy_sem.at[h, j], at_y(via * f), 4)
        yield at("a3", h)
        arrived(fresh.at[h, 0], keep_sem.at[h, 0])
        for k, i in ((-1, 2), (1, 3), (-3, 4), (3, 5), (4, 6)):
            arrived(out_x(h, x, ys(k * f)), gsy_sem.at[h, i])
        send(all_x(h, x), all_x(h, x), gx_sem.at[h, 0], at_x(f), 32)
        send(all_x(h, x), all_x(h, x), gx_sem.at[h, 2], at_x(-f), 32)
        yield at("a4", h)
        chunk = all_x(h, xs(-f))
        arrived(chunk, gx_sem.at[h, 0])
        send(chunk, chunk, gx_sem.at[h, 1], at_x(f), 32)
        yield at("a5", h)
        arrived(all_x(h, xs(f)), gx_sem.at[h, 2])
        arrived(all_x(h, xs(2)), gx_sem.at[h, 1])

    in_order(both_cores(0), both_cores(1), y_back(0), y_back(1), x_back(0), x_back(1))
    finish()


def local(partials, params, left_basis, right_basis, first_moment, second_moment, owner_list):
    dma = pltpu.SemaphoreType.DMA
    full = (256, 256)
    vm = pltpu.VMEM
    any_spec = pl.BlockSpec(memory_space=pl.ANY)
    in_hbm = functools.partial(pltpu.with_memory_space_constraint, memory_space=pltpu.HBM)
    updated, first_out, second_out = pl.pallas_call(
        body,
        out_shape=(
            pltpu.VMEM((8, NY, NX, 8, 256), F32),
            pltpu.VMEM(full, F32),
            pltpu.VMEM(full, F32),
        ),
        in_specs=[any_spec] * 7,
        out_specs=(any_spec,) * 3,
        scratch_shapes=[
            vm((1, 128), jnp.int32), pltpu.SMEM((1, 128), jnp.int32), vm((ND, 128), jnp.int32), pltpu.SMEM((ND, 128), jnp.int32),
            vm((8, 256, 256), BF16), vm((8, 8, 256), F32),
            vm(full, F32), vm(full, F32), vm(full, F32), vm(full, F32), vm(full, F32), vm(full, F32),
            vm((2, NX, 4, NY, 8, 128), F32), vm((2, NY, 4, NX, 8, 128), F32),
            vm((2, 3, 4, NY, 8, 128), F32), vm((2, 7, 4, NX, 8, 128), F32),
            vm((2, NX - 1, 4, 8, 128), F32), vm((2, NY - 1, 4, 8, 128), F32),
            vm((2, NC, NZ, 4, 8, 128), F32), vm((2, NC, NZ, 4, 8, 128), F32),
            vm((2, ND, 8, 128), F32), vm((2, ND, 8, 128), F32),
            vm((2, ND, 8, 128), F32), vm((NC, ND, 8, 128), F32), vm((NC, ND, 8, 128), F32),
            vm((2, 2, NZ, 4, 8, 128), F32),
            vm((2, 2, NZ - 1, 4, 8, 128), F32), vm((2, 2, 4, 8, 128), F32),
            vm(full, BF16), vm(full, BF16), vm(full, BF16), vm(full, BF16),
            vm(full, BF16), vm(full, BF16), vm(full, BF16), vm(full, BF16),
            vm((3072, 8, 128), F32),
            dma((9,)), dma((1,)), dma((1,)), dma((2, 3)), dma((2, 7)), dma((2,)), dma((2,)), dma((2, 2, 7)), dma((2, 2)),
            dma((2,)), dma((2,)), dma((2,)), dma((2, 2, 7)), dma((2, 7)), dma((2,)), dma((2, 3)), dma((2, 7)), dma((2, 2)),
            dma((2,)),
        ],
        compiler_params=pltpu.CompilerParams(
            collective_id=0, has_side_effects=True, vmem_limit_bytes=48 * 1024 * 1024
        ),
        name="soap_step",
    )(
        *map(
            in_hbm,
            (
                owner_list.reshape(1, 128), partials[0], params, left_basis[0, 0, 0], right_basis[0, 0, 0],
                first_moment[0, 0, 0], second_moment[0, 0, 0],
            ),
        )
    )
    return (
        updated.reshape(8, 256, 256),
        first_out[None, None, None],
        second_out[None, None, None],
    )


def solution(mesh):
    return jax.shard_map(
        local,
        mesh=mesh,
        in_specs=(
            P("dp", "shard", None, None),
            P("shard", "dp", None),
            P("dp", "shard", None, None, None),
            P("dp", "shard", None, None, None),
            P("dp", "shard", None, None, None),
            P("dp", "shard", None, None, None),
            P(),
        ),
        out_specs=(
            P("shard", None, None),
            P("dp", "shard", None, None, None),
            P("dp", "shard", None, None, None),
        ),
        check_vma=False,
    )
```
